32 devices in a mesh: ctx: 8 (over z, y), head: 4 (over x, core).
Axes of the slice: x: 2, y: 2, z: 4, core: 2. Of those that a mesh axis runs over, the one named last changes fastest.
Arguments:
- queries: bfloat16 [2048, 4096], P('ctx', 'head'), may hold values from -48 to 48
- enc_keys: bfloat16 [256, 4096], P('ctx', 'head'), may hold values from -4 to 4
- enc_values: bfloat16 [256, 4096], P('ctx', 'head'), may hold values from -6 to 6
- grad_out: bfloat16 [2048, 4096], P('ctx', 'head'), may hold values from -48 to 48
- out_weight: bfloat16 [4096, 4096], P('head'), may hold values from -0.09375 to 0.09375
Outputs:
- query_grad: bfloat16 [2048, 4096], P('ctx', 'head')
- key_grad: bfloat16 [256, 4096], P('ctx', 'head')
- value_grad: bfloat16 [256, 4096], P('ctx', 'head')
The draws below stay inside these ranges and needn't reach their ends.
All inputs are finite; a program needn't handle non-finite values.
Results may differ from the reference program's by a relative error of at most 0.0085.
Values may be sent and summed in bfloat16 or wider, within the bound.
A program may use at most 64 MiB of HBM per device.

```python
import jax
import jax.numpy as jnp
from jax import lax

D = 4096
HEADS = 64
DH = 64
INNER = 4096
LQ = 2048
LK = 256


def drawn_pair(key):
    query_key = jax.random.fold_in(key, 11)
    entry_key = jax.random.fold_in(key, 12)
    inner_width = HEADS * DH
    queries = jnp.clip(jax.random.normal(query_key, (LQ, inner_width), jnp.float32), -4.0, 4.0)
    keys_all = jnp.clip(jax.random.normal(entry_key, (LK, inner_width), jnp.float32), -4.0, 4.0)
    return (queries, keys_all)


def draw_queries(key, part):
    return drawn_pair(jax.random.fold_in(key, 7))[0].astype(jnp.bfloat16)


def draw_enc_keys(key, part):
    return drawn_pair(jax.random.fold_in(key, 7))[1].astype(jnp.bfloat16)


def block_scale(rng, extent, shards, smallest, largest):
    loudness = 1.0
    for position, shards_of in shards:
        heights = jax.random.uniform(jax.random.fold_in(jax.random.fold_in(rng, 6), position), (shards_of,), jnp.float32, smallest / len(shards), largest / len(shards))
        loudness = loudness * jnp.repeat(jnp.exp(heights), extent[position] // shards_of).reshape((-1,) + (1,) * (len(extent) - 1 - position))
    return loudness


def noise(rng, shape, deviation, reach, pieces=(), held_as=jnp.bfloat16):
    factor_of = block_scale(rng, shape, pieces, -0.22, 0.18) if pieces else 1.0
    values = jax.random.normal(rng, shape, jnp.float32) * deviation * factor_of
    return jnp.minimum(jnp.maximum(values, -reach), reach).astype(held_as)


def setup_inputs(seed: int = 0) -> dict:
    streams_of = jax.random.split(jax.random.key(seed), 6)
    return {
        "queries": draw_queries(jax.random.fold_in(streams_of[5], 71), 0),
        "enc_keys": draw_enc_keys(jax.random.fold_in(streams_of[5], 71), 0),
        "enc_values": noise(streams_of[2], (LK, INNER), 1.0, 6.0, ((0, 8), (1, 4))),
        "grad_out": noise(streams_of[3], (LQ, D), 8.0, 48.0, ((0, 8), (1, 4))),
        "out_weight": noise(streams_of[4], (INNER, D), D ** -0.5, 0.09375, ((0, 4),)),
    }


def by_head(array, length):
    return array.reshape(length, HEADS, DH).transpose(1, 0, 2)


def merged(array, length):
    return array.transpose(1, 0, 2).reshape(length, HEADS * DH).astype(jnp.bfloat16)


def reference(queries, enc_keys, enc_values, grad_out, out_weight):
    head_grads = jnp.dot(grad_out, out_weight.T, preferred_element_type=jnp.float32).astype(jnp.bfloat16)
    score_scale = DH ** -0.5

    def one_head(operands):
        query_head, key_head, value_head, grad_head = operands
        scores = score_scale * jnp.dot(query_head, key_head.T, preferred_element_type=jnp.float32)
        row_top = jnp.max(scores, axis=1, keepdims=True)
        exponent = jnp.exp(scores - row_top)
        attention = exponent / jnp.sum(exponent, axis=1, keepdims=True)
        attention_low = attention.astype(jnp.bfloat16)
        attended = jnp.dot(attention_low, value_head, preferred_element_type=jnp.float32)
        row_delta = jnp.sum(grad_head.astype(jnp.float32) * attended, axis=1, keepdims=True)
        prob_grad = jnp.dot(grad_head, value_head.T, preferred_element_type=jnp.float32)
        score_grad = (score_scale * attention * (prob_grad - row_delta)).astype(jnp.bfloat16)
        query_part = jnp.dot(score_grad, key_head, preferred_element_type=jnp.float32)
        key_part = jnp.dot(score_grad.T, query_head, preferred_element_type=jnp.float32)
        value_part = jnp.dot(attention_low.T, grad_head, preferred_element_type=jnp.float32)
        return query_part, key_part, value_part

    query_all, key_all, value_all = lax.map(
        one_head,
        (by_head(queries, LQ), by_head(enc_keys, LK), by_head(enc_values, LK), by_head(head_grads, LQ)),
    )
    return merged(query_all, LQ), merged(key_all, LK), merged(value_all, LK)
```

```python
import functools

import jax
import jax.numpy as jnp
from jax import lax
from jax.experimental import pallas as pl
from jax.experimental.pallas import tpu as pltpu
from jax.sharding import PartitionSpec as P

DH = 64
PAIR = 2 * DH
MESH = pl.DeviceIdType.MESH
NT = (((1,), (1,)), ((), ()))
NN = (((1,), (0,)), ((), ()))


def dot(a, b, dims):
    return lax.dot_general(a, b, dims, preferred_element_type=jnp.float32)


def inner_extent(n):
    best = 1
    while n % (2 * best) == 0 and (2 * best) ** 2 <= n:
        best *= 2
    return best


def kernel(Z, Y, X, C, kc, q_hbm, k_hbm, v_hbm, g_hbm, w_hbm, dq_ref, dk_ref, dv_ref,
           qbuf, q2buf, kvbuf, ktbuf, gbuf, wbuf, acc, dobuf, pbuf, dsbuf, part, s1, r1, s2, r2,
           loc_sem, w_sem, g_recv, gx_send, gc_send, gf_send, kv_recv, kvz_send, kvy_send, kvf_send,
           s1_send, r1_recv, s2_send, r2_recv):
    rows, width = q_hbm.shape
    r = k_hbm.shape[0]
    keys = Z * Y * r
    half = Z * r
    pairs = width // PAIR
    chunks = width // kc
    c = lax.axis_index("ctx")
    h = lax.axis_index("head")
    z, y = c // Y, c % Y
    x, k = h // C, h % C

    def at_z(b):
        return {"ctx": lax.rem(z + b, Z) * Y + y, "head": h}

    def at_y(a):
        return {"ctx": z * Y + lax.rem(y + a, Y), "head": h}

    def at_x(d):
        return {"ctx": c, "head": lax.rem(x + d, X) * C + k}

    def at_core(d):
        return {"ctx": c, "head": x * C + lax.rem(k + d, C)}

    def remote(src, dst, send, recv, target):
        return pltpu.make_async_remote_copy(
            src_ref=src, dst_ref=dst, send_sem=send, recv_sem=recv,
            device_id=target, device_id_type=MESH)

    def slot(a, b):
        return pl.ds((a * Z + b) * r, r)

    kv_hbm = (k_hbm, v_hbm)

    loads = [
        pltpu.make_async_copy(g_hbm, gbuf.at[0, 0], loc_sem.at[0]),
        pltpu.make_async_copy(q_hbm, qbuf, loc_sem.at[1]),
        pltpu.make_async_copy(k_hbm, kvbuf.at[0, slot(0, 0)], loc_sem.at[2]),
        pltpu.make_async_copy(v_hbm, kvbuf.at[1, slot(0, 0)], loc_sem.at[3]),
    ]

    def w_load(d, e):
        block = lax.rem(x + d, X) * C + lax.rem(k + e, C)
        cols = pl.ds(pl.multiple_of(block * width, width), width)
        return pltpu.make_async_copy(w_hbm.at[:, cols], wbuf.at[d, e], w_sem.at[d, e])

    loads[0].start()
    w_load(0, 0).start()
    for copy in loads[1:]:
        copy.start()
    for d in range(X):
        for e in range(C):
            if d + e:
                w_load(d, e).start()

    partners = ([at_z(b) for b in range(1, Z)] + [at_y(a) for a in range(1, Y)]
                + [at_x(d) for d in range(1, X)] + [at_core(d) for d in range(1, C)])
    barrier = pltpu.get_barrier_semaphore()
    for target in partners:
        pl.semaphore_signal(barrier, inc=1, device_id=target, device_id_type=MESH)
    pl.semaphore_wait(barrier, len(partners))

    def cols(j):
        return pl.ds(j * kc, kc)

    def gx(d, j):
        return remote(g_hbm.at[:, cols(j)], gbuf.at[X - d, 0, :, cols(j)],
                      gx_send.at[d, j], g_recv.at[X - d, 0, j], at_x(d))

    def gc(e):
        return remote(g_hbm, gbuf.at[0, C - e], gc_send.at[e], g_recv.at[0, C - e, 0], at_core(e))

    def gf(d, e, j):
        return remote(gbuf.at[d, 0, :, cols(j)], gbuf.at[d, C - e, :, cols(j)],
                      gf_send.at[d, e, j], g_recv.at[d, C - e, j], at_core(e))

    def kvz(t, b):
        return remote(kv_hbm[t], kvbuf.at[t, slot(0, Z - b)],
                      kvz_send.at[t, b], kv_recv.at[t, 0, Z - b], at_z(b))

    def kvy(t, a):
        return remote(kv_hbm[t], kvbuf.at[t, slot(Y - a, 0)],
                      kvy_send.at[t, a], kv_recv.at[t, Y - a, 0], at_y(a))

    def kvf(t, a, b):
        return remote(kvbuf.at[t, slot(0, b)], kvbuf.at[t, slot(Y - a, b)],
                      kvf_send.at[t, a, b], kv_recv.at[t, Y - a, b], at_y(a))

    for d in range(1, X):
        gx(d, 0).start()
    for t in range(2):
        for b in range(1, Z):
            kvz(t, b).start()
        for a in range(1, Y):
            kvy(t, a).start()
    for j in range(1, chunks):
        for d in range(1, X):
            gx(d, j).start()
    for e in range(1, C):
        gc(e).start()

    def forward_g(j):
        for d in range(1, X):
            gx(X - d, j).wait_recv()
            for e in range(1, C):
                gf(d, e, j).start()

    def forward_kv(t):
        for b in range(1, Z):
            kvz(t, Z - b).wait_recv()
            for a in range(1, Y):
                kvf(t, a, b).start()

    def arrived_kv(t):
        for a in range(1, Y):
            kvy(t, Y - a).wait_recv()
            for b in range(1, Z):
                kvf(t, Y - a, b).wait_recv()

    def add_chunk(j):
        total = acc[...]
        for d in range(1, X):
            for e in range(C):
                if e:
                    gf(d, C - e, j).wait_recv()
                total += dot(gbuf[d, e, :, j * kc:(j + 1) * kc], wbuf[d, e, :, j * kc:(j + 1) * kc], NT)
        acc[...] = total

    loads[0].wait()
    w_load(0, 0).wait()
    acc[...] = dot(gbuf[0, 0], wbuf[0, 0], NT)
    for e in range(1, C):
        gc(C - e).wait_recv()
        w_load(0, e).wait()
        acc[...] += dot(gbuf[0, e], wbuf[0, e], NT)
    for d in range(1, X):
        for e in range(C):
            w_load(d, e).wait()

    lane = lax.broadcasted_iota(jnp.int32, (1, PAIR), 1)
    low = jnp.where(lane < DH, 1.0, 0.0).astype(jnp.bfloat16)
    high = jnp.where(lane < DH, 0.0, 1.0).astype(jnp.bfloat16)
    scale = DH ** -0.5

    def at_pair(p):
        return pl.ds(pl.multiple_of(p * PAIR, PAIR), PAIR)

    def both_heads(block):
        return jnp.concatenate((block * low, block * high), axis=0)

    def attention(p, carry):
        q2 = both_heads(qbuf[:, at_pair(p)] * jnp.bfloat16(scale))
        q2buf[p] = q2
        key_pair = kvbuf[0, :, at_pair(p)]
        ktbuf[p] = key_pair.astype(jnp.float32).T.astype(jnp.bfloat16)
        scores = dot(key_pair, q2, NT)
        exponent = jnp.exp(scores - jnp.max(scores, axis=0, keepdims=True))
        pbuf[p] = exponent * (1.0 / jnp.sum(exponent, axis=0, keepdims=True))
        return carry

    loads[1].wait()
    loads[2].wait()
    forward_g(0)
    forward_kv(0)
    done = 0
    for j in range(1, chunks):
        if j == 1:
            arrived_kv(0)
        forward_g(j)
        if j == min(2, chunks - 1):
            forward_kv(1)
        add_chunk(j - 1)
        upto = pairs * j // (chunks - 1)
        lax.fori_loop(done, upto, attention, 0)
        done = upto
    if chunks == 1:
        arrived_kv(0)
        forward_kv(1)
        lax.fori_loop(0, pairs, attention, 0)
    add_chunk(chunks - 1)
    dobuf[...] = acc[...].astype(jnp.bfloat16)
    loads[3].wait()
    arrived_kv(1)

    def send1(a, p):
        return remote(s1.at[a - 1, p], r1.at[Y - a - 1, p], s1_send.at[a - 1, p],
                      r1_recv.at[Y - a - 1, p], at_y(a))

    def send2(b, p):
        return remote(s2.at[b - 1, p], r2.at[Z - b - 1, p], s2_send.at[b - 1, p],
                      r2_recv.at[Z - b - 1, p], at_z(b))

    def terms(p):
        do2 = both_heads(dobuf[:, at_pair(p)])
        prob = pbuf[p]
        prob_low = prob.astype(jnp.bfloat16)
        dp = dot(kvbuf[1, :, at_pair(p)], do2, NT)
        delta = jnp.sum(prob_low.astype(jnp.float32) * dp, axis=0, keepdims=True)
        ds = (prob * (dp - delta)).astype(jnp.bfloat16)
        dsbuf[p] = ds
        for t, term in enumerate((dot(ds, q2buf[p], NN), dot(prob_low, do2, NN))):
            part[p, t] = term[:half]
            for a in range(1, Y):
                s1[a - 1, p, t] = term[a * half:(a + 1) * half].astype(jnp.bfloat16)
        for a in range(1, Y):
            send1(a, p).start()

    def second(p):
        for a in range(1, Y):
            send1(Y - a, p).wait_recv()
        for t in range(2):
            total = part[p, t]
            for a in range(1, Y):
                total += r1[a - 1, p, t].astype(jnp.float32)
            part[p, t, :r] = total[:r]
            for b in range(1, Z):
                s2[b - 1, p, t] = total[b * r:(b + 1) * r].astype(jnp.bfloat16)
        for b in range(1, Z):
            send2(b, p).start()

    def query_part(p):
        dqt = dot(ktbuf[p], dsbuf[p], NN)
        both = jnp.concatenate((dqt[:DH, :rows], dqt[DH:, rows:]), axis=0)
        dq_ref[:, at_pair(p)] = (both.T * scale).astype(jnp.bfloat16)

    lag = min(2, pairs)

    def first_loop(p, carry):
        terms(p)

        @pl.when(p >= lag)
        def _():
            second(p - lag)
        return carry

    lax.fori_loop(0, pairs, first_loop, 0)

    def tail_loop(p, carry):
        query_part(p)

        @pl.when(p >= pairs - lag)
        def _():
            second(p)
        return carry

    lax.fori_loop(0, pairs, tail_loop, 0)

    def final_loop(p, carry):
        for b in range(1, Z):
            send2(Z - b, p).wait_recv()
        for t, out in enumerate((dk_ref, dv_ref)):
            total = part[p, t, :r]
            for b in range(1, Z):
                total += r2[b - 1, p, t].astype(jnp.float32)
            out[:, at_pair(p)] = total.astype(jnp.bfloat16)
        for a in range(1, Y):
            send1(a, p).wait_send()
        for b in range(1, Z):
            send2(b, p).wait_send()
        return carry

    lax.fori_loop(0, pairs, final_loop, 0)

    for j in range(chunks):
        for d in range(1, X):
            gx(d, j).wait_send()
            for e in range(1, C):
                gf(d, e, j).wait_send()
    for e in range(1, C):
        gc(e).wait_send()
    for t in range(2):
        for b in range(1, Z):
            kvz(t, b).wait_send()
            for a in range(1, Y):
                kvf(t, a, b).wait_send()
        for a in range(1, Y):
            kvy(t, a).wait_send()


def local(n, m, queries, enc_keys, enc_values, grad_out, out_weight):
    rows, width = queries.shape
    r = enc_keys.shape[0]
    Y = inner_extent(n)
    Z = n // Y
    C = 2 if m % 2 == 0 else 1
    X = m // C
    kc = min(256, width)
    pairs = width // PAIR
    chunks = width // kc
    keys, half = n * r, Z * r
    low, full = jnp.bfloat16, jnp.float32
    y1, z1 = max(Y - 1, 1), max(Z - 1, 1)
    dma = pltpu.SemaphoreType.DMA
    vmem = pltpu.VMEM
    return pl.pallas_call(
        functools.partial(kernel, Z, Y, X, C, kc),
        out_shape=(
            jax.ShapeDtypeStruct((rows, width), low),
            jax.ShapeDtypeStruct((r, width), low),
            jax.ShapeDtypeStruct((r, width), low),
        ),
        in_specs=[pl.BlockSpec(memory_space=pl.ANY)] * 5,
        out_specs=[pl.BlockSpec(memory_space=pltpu.VMEM)] * 3,
        scratch_shapes=[
            vmem((rows, width), low),
            vmem((pairs, 2 * rows, PAIR), low),
            vmem((2, keys, width), low),
            vmem((pairs, PAIR, keys), low),
            vmem((X, C, rows, width), low),
            vmem((X, C, width, width), low),
            vmem((rows, width), full),
            vmem((rows, width), low),
            vmem((pairs, keys, 2 * rows), full),
            vmem((pairs, keys, 2 * rows), low),
            vmem((pairs, 2, half, PAIR), full),
            vmem((y1, pairs, 2, half, PAIR), low),
            vmem((y1, pairs, 2, half, PAIR), low),
            vmem((z1, pairs, 2, r, PAIR), low),
            vmem((z1, pairs, 2, r, PAIR), low),
            dma((4,)),
            dma((X, C)),
            dma((X, C, chunks)),
            dma((X, chunks)),
            dma((C,)),
            dma((X, C, chunks)),
            dma((2, Y, Z)),
            dma((2, Z)),
            dma((2, Y)),
            dma((2, Y, Z)),
            dma((y1, pairs)),
            dma((y1, pairs)),
            dma((z1, pairs)),
            dma((z1, pairs)),
        ],
        compiler_params=pltpu.CompilerParams(
            collective_id=0, has_side_effects=True, vmem_limit_bytes=52 * 1024 * 1024),
    )(queries, enc_keys, enc_values, grad_out, out_weight)


def solution(mesh):
    return jax.shard_map(
        functools.partial(local, mesh.shape["ctx"], mesh.shape["head"]),
        mesh=mesh,
        in_specs=(
            P("ctx", "head"),
            P("ctx", "head"),
            P("ctx", "head"),
            P("ctx", "head"),
            P("head", None),
        ),
        out_specs=(P("ctx", "head"), P("ctx", "head"), P("ctx", "head")),
        check_vma=False,
    )
```

```python
import functools

import jax
import jax.numpy as jnp
from jax import lax
from jax.experimental import pallas as pl
from jax.experimental.pallas import tpu as pltpu
from jax.sharding import PartitionSpec as P

DH = 64
PAIR = 2 * DH
MESH = pl.DeviceIdType.MESH
NT = (((1,), (1,)), ((), ()))
NN = (((1,), (0,)), ((), ()))


def dot(a, b, dims):
    return lax.dot_general(a, b, dims, preferred_element_type=jnp.float32)


def inner_extent(n):
    best = 1
    while n % (2 * best) == 0 and (2 * best) ** 2 <= n:
        best *= 2
    return best


def kernel(Z, Y, X, C, kc, q_hbm, k_hbm, v_hbm, g_hbm, w_hbm, dq_ref, dk_ref, dv_ref,
           qbuf, q2buf, kvbuf, ktbuf, gbuf, wbuf, acc, dobuf, pbuf, dsbuf, part, s1, r1, s2, r2,
           loc_sem, w_sem, g_recv, gx_send, gc_send, gf_send, kv_recv, kvz_send, kvy_send, kvf_send,
           s1_send, r1_recv, s2_send, r2_recv):
    rows, width = q_hbm.shape
    r = k_hbm.shape[0]
    keys = Z * Y * r
    half = Z * r
    pairs = width // PAIR
    chunks = width // kc
    group = 2 if pairs % 2 == 0 else 1
    groups = pairs // group
    c = lax.axis_index("ctx")
    h = lax.axis_index("head")
    z, y = c // Y, c % Y
    x, k = h // C, h % C

    def at_z(b):
        return {"ctx": lax.rem(z + b, Z) * Y + y, "head": h}

    def at_y(a):
        return {"ctx": z * Y + lax.rem(y + a, Y), "head": h}

    def at_x(d):
        return {"ctx": c, "head": lax.rem(x + d, X) * C + k}

    def at_core(d):
        return {"ctx": c, "head": x * C + lax.rem(k + d, C)}

    def remote(src, dst, send, recv, target):
        return pltpu.make_async_remote_copy(
            src_ref=src, dst_ref=dst, send_sem=send, recv_sem=recv,
            device_id=target, device_id_type=MESH)

    def slot(a, b):
        return pl.ds((a * Z + b) * r, r)

    kv_hbm = (k_hbm, v_hbm)

    loads = [
        pltpu.make_async_copy(g_hbm, gbuf.at[0, 0], loc_sem.at[0]),
        pltpu.make_async_copy(q_hbm, qbuf, loc_sem.at[1]),
        pltpu.make_async_copy(k_hbm, kvbuf.at[0, slot(0, 0)], loc_sem.at[2]),
        pltpu.make_async_copy(v_hbm, kvbuf.at[1, slot(0, 0)], loc_sem.at[3]),
    ]

    def w_load(d, e):
        block = lax.rem(x + d, X) * C + lax.rem(k + e, C)
        cols = pl.ds(pl.multiple_of(block * width, width), width)
        return pltpu.make_async_copy(w_hbm.at[:, cols], wbuf.at[d, e], w_sem.at[d, e])

    partners = ([at_z(b) for b in range(1, Z)] + [at_y(a) for a in range(1, Y)]
                + [at_x(d) for d in range(1, X)] + [at_core(d) for d in range(1, C)])
    barrier = pltpu.get_barrier_semaphore()
    for target in partners:
        pl.semaphore_signal(barrier, inc=1, device_id=target, device_id_type=MESH)
    loads[0].start()
    w_load(0, 0).start()
    pl.semaphore_wait(barrier, len(partners))

    def cols(j):
        return pl.ds(j * kc, kc)

    def gx(d, j):
        return remote(g_hbm.at[:, cols(j)], gbuf.at[X - d, 0, :, cols(j)],
                      gx_send.at[d, j], g_recv.at[X - d, 0, j], at_x(d))

    def gc(e):
        return remote(g_hbm, gbuf.at[0, C - e], gc_send.at[e], g_recv.at[0, C - e, 0], at_core(e))

    def gf(d, e, j):
        return remote(gbuf.at[d, 0, :, cols(j)], gbuf.at[d, C - e, :, cols(j)],
                      gf_send.at[d, e, j], g_recv.at[d, C - e, j], at_core(e))

    def kvz(t, b):
        return remote(kv_hbm[t], kvbuf.at[t, slot(0, Z - b)],
                      kvz_send.at[t, b], kv_recv.at[t, 0, Z - b], at_z(b))

    def kvy(t, a):
        return remote(kv_hbm[t], kvbuf.at[t, slot(Y - a, 0)],
                      kvy_send.at[t, a], kv_recv.at[t, Y - a, 0], at_y(a))

    def kvf(t, a, b):
        return remote(kvbuf.at[t, slot(0, b)], kvbuf.at[t, slot(Y - a, b)],
                      kvf_send.at[t, a, b], kv_recv.at[t, Y - a, b], at_y(a))

    def start_kv(t):
        for b in range(1, Z):
            kvz(t, Z - b).start()
        for a in range(1, Y):
            kvy(t, a).start()

    for d in range(1, X):
        gx(d, 0).start()
    start_kv(0)
    for e in range(1, C):
        gc(e).start()
    for j in range(1, chunks):
        for d in range(1, X):
            gx(d, j).start()
    for copy in loads[1:]:
        copy.start()
    for d in range(X):
        for e in range(C):
            if d + e:
                w_load(d, e).start()

    def forward_g(j):
        for d in range(1, X):
            gx(X - d, j).wait_recv()
            for e in range(1, C):
                gf(d, e, j).start()

    nearest = sorted(range(1, Z), key=lambda b: min(b, Z - b))

    def forward_kv(t):
        for i, b in enumerate(nearest):
            kvz(t, Z - b).wait_recv()
            for a in range(1, Y):
                kvf(t, a, b).start()
            if t == 0 and i == 0:
                start_kv(1)
        if t == 0 and not nearest:
            start_kv(1)

    def arrived_kv(t):
        for a in range(1, Y):
            kvy(t, Y - a).wait_recv()
            for b in range(1, Z):
                kvf(t, Y - a, b).wait_recv()

    def add_chunks(first, last):
        span = slice(first * kc, last * kc)
        total = acc[...]
        for d in range(1, X):
            for e in range(C):
                if e:
                    for j in range(first, last):
                        gf(d, C - e, j).wait_recv()
                total += dot(gbuf[d, e, :, span], wbuf[d, e, :, span], NT)
        acc[...] = total

    loads[0].wait()
    w_load(0, 0).wait()
    acc[...] = dot(gbuf[0, 0], wbuf[0, 0], NT)
    for e in range(1, C):
        gc(C - e).wait_recv()
        w_load(0, e).wait()
        acc[...] += dot(gbuf[0, e], wbuf[0, e], NT)
    for d in range(1, X):
        for e in range(C):
            w_load(d, e).wait()

    lane = lax.broadcasted_iota(jnp.int32, (1, PAIR), 1)
    low = jnp.where(lane < DH, 1.0, 0.0).astype(jnp.bfloat16)
    high = jnp.where(lane < DH, 0.0, 1.0).astype(jnp.bfloat16)
    scale = DH ** -0.5

    def at_pair(p):
        return pl.ds(pl.multiple_of(p * PAIR, PAIR), PAIR)

    def both_heads(block):
        return jnp.concatenate((block * low, block * high), axis=0)

    def attention(g, carry):
        members = [g * group + i for i in range(group)]
        queries = [both_heads(qbuf[:, at_pair(p)] * jnp.bfloat16(scale)) for p in members]
        key_pairs = [kvbuf[0, :, at_pair(p)] for p in members]
        scores = [dot(a, b, NT) for a, b in zip(key_pairs, queries)]
        exponents = [jnp.exp(s - jnp.max(s, axis=0, keepdims=True)) for s in scores]
        probs = [e * (1.0 / jnp.sum(e, axis=0, keepdims=True)) for e in exponents]
        for p, q2, key_pair, prob in zip(members, queries, key_pairs, probs):
            q2buf[p] = q2
            ktbuf[p] = key_pair.astype(jnp.float32).T.astype(jnp.bfloat16)
            pbuf[p] = prob
        return carry

    def attend(first, last):
        if first < last:
            lax.fori_loop(first, last, attention, 0)

    loads[1].wait()
    loads[2].wait()
    forward_kv(0)
    forward_g(0)
    if chunks > 1:
        forward_g(1)
        add_chunks(0, 1)
    arrived_kv(0)
    attend(0, groups // 4)
    if chunks > 2:
        forward_g(2)
    attend(groups // 4, groups // 2)
    forward_kv(1)
    for j in range(3, chunks):
        forward_g(j)
    attend(groups // 2, 3 * groups // 4)
    if chunks > 2:
        add_chunks(1, chunks - 1)
    attend(3 * groups // 4, groups)
    add_chunks(chunks - 1, chunks)
    dobuf[...] = acc[...].astype(jnp.bfloat16)
    loads[3].wait()
    arrived_kv(1)

    def send1(a, p):
        return remote(s1.at[a - 1, p], r1.at[Y - a - 1, p], s1_send.at[a - 1, p],
                      r1_recv.at[Y - a - 1, p], at_y(a))

    def send2(b, p):
        return remote(s2.at[b - 1, p], r2.at[Z - b - 1, p], s2_send.at[b - 1, p],
                      r2_recv.at[Z - b - 1, p], at_z(b))

    def terms(g):
        members = [g * group + i for i in range(group)]
        grads = [both_heads(dobuf[:, at_pair(p)]) for p in members]
        dps = [dot(kvbuf[1, :, at_pair(p)], do2, NT) for p, do2 in zip(members, grads)]
        probs = [pbuf[p] for p in members]
        lows = [prob.astype(jnp.bfloat16) for prob in probs]
        deltas = [jnp.sum(a.astype(jnp.float32) * b, axis=0, keepdims=True) for a, b in zip(lows, dps)]
        scored = [(a * (b - d)).astype(jnp.bfloat16) for a, b, d in zip(probs, dps, deltas)]
        value_terms = [dot(a, b, NN) for a, b in zip(lows, grads)]
        key_terms = [dot(ds, q2buf[p], NN) for ds, p in zip(scored, members)]
        for p, ds, key_term, value_term in zip(members, scored, key_terms, value_terms):
            dsbuf[p] = ds
            for t, term in enumerate((key_term, value_term)):
                part[p, t] = term[:half]
                for a in range(1, Y):
                    s1[a - 1, p, t] = term[a * half:(a + 1) * half].astype(jnp.bfloat16)
        for p in members:
            for a in range(1, Y):
                send1(a, p).start()

    def second(p):
        for a in range(1, Y):
            send1(Y - a, p).wait_recv()
        for t in range(2):
            total = part[p, t]
            for a in range(1, Y):
                total += r1[a - 1, p, t].astype(jnp.float32)
            part[p, t, :r] = total[:r]
            for b in range(1, Z):
                s2[b - 1, p, t] = total[b * r:(b + 1) * r].astype(jnp.bfloat16)
        for b in range(1, Z):
            send2(b, p).start()

    def query_part(p):
        dqt = dot(ktbuf[p], dsbuf[p], NN)
        both = jnp.concatenate((dqt[:DH, :rows], dqt[DH:, rows:]), axis=0)
        dq_ref[:, at_pair(p)] = (both.T * scale).astype(jnp.bfloat16)

    def relay(g):
        for i in range(group):
            query_part(g * group + i)
            second(g * group + i)

    def first_loop(g, carry):
        terms(g)

        @pl.when(g >= 1)
        def _():
            relay(g - 1)
        return carry

    lax.fori_loop(0, groups, first_loop, 0)
    relay(groups - 1)

    def final_loop(p, carry):
        for b in range(1, Z):
            send2(Z - b, p).wait_recv()
        for t, out in enumerate((dk_ref, dv_ref)):
            total = part[p, t, :r]
            for b in range(1, Z):
                total += r2[b - 1, p, t].astype(jnp.float32)
            out[:, at_pair(p)] = total.astype(jnp.bfloat16)
        for a in range(1, Y):
            send1(a, p).wait_send()
        for b in range(1, Z):
            send2(b, p).wait_send()
        return carry

    lax.fori_loop(0, pairs, final_loop, 0)

    for j in range(chunks):
        for d in range(1, X):
            gx(d, j).wait_send()
            for e in range(1, C):
                gf(d, e, j).wait_send()
    for e in range(1, C):
        gc(e).wait_send()
    for t in range(2):
        for b in range(1, Z):
            kvz(t, b).wait_send()
            for a in range(1, Y):
                kvf(t, a, b).wait_send()
        for a in range(1, Y):
            kvy(t, a).wait_send()


def local(n, m, queries, enc_keys, enc_values, grad_out, out_weight):
    rows, width = queries.shape
    r = enc_keys.shape[0]
    Y = inner_extent(n)
    Z = n // Y
    C = 2 if m % 2 == 0 else 1
    X = m // C
    kc = min(256, width)
    pairs = width // PAIR
    chunks = width // kc
    keys, half = n * r, Z * r
    low, full = jnp.bfloat16, jnp.float32
    y1, z1 = max(Y - 1, 1), max(Z - 1, 1)
    dma = pltpu.SemaphoreType.DMA
    vmem = pltpu.VMEM
    return pl.pallas_call(
        functools.partial(kernel, Z, Y, X, C, kc),
        out_shape=(
            jax.ShapeDtypeStruct((rows, width), low),
            jax.ShapeDtypeStruct((r, width), low),
            jax.ShapeDtypeStruct((r, width), low),
        ),
        in_specs=[pl.BlockSpec(memory_space=pl.ANY)] * 5,
        out_specs=[pl.BlockSpec(memory_space=pltpu.VMEM)] * 3,
        scratch_shapes=[
            vmem((rows, width), low),
            vmem((pairs, 2 * rows, PAIR), low),
            vmem((2, keys, width), low),
            vmem((pairs, PAIR, keys), low),
            vmem((X, C, rows, width), low),
            vmem((X, C, width, width), low),
            vmem((rows, width), full),
            vmem((rows, width), low),
            vmem((pairs, keys, 2 * rows), full),
            vmem((pairs, keys, 2 * rows), low),
            vmem((pairs, 2, half, PAIR), full),
            vmem((y1, pairs, 2, half, PAIR), low),
            vmem((y1, pairs, 2, half, PAIR), low),
            vmem((z1, pairs, 2, r, PAIR), low),
            vmem((z1, pairs, 2, r, PAIR), low),
            dma((4,)),
            dma((X, C)),
            dma((X, C, chunks)),
            dma((X, chunks)),
            dma((C,)),
            dma((X, C, chunks)),
            dma((2, Y, Z)),
            dma((2, Z)),
            dma((2, Y)),
            dma((2, Y, Z)),
            dma((y1, pairs)),
            dma((y1, pairs)),
            dma((z1, pairs)),
            dma((z1, pairs)),
        ],
        compiler_params=pltpu.CompilerParams(
            collective_id=0, has_side_effects=True, vmem_limit_bytes=62 * 1024 * 1024),
    )(queries, enc_keys, enc_values, grad_out, out_weight)


def solution(mesh):
    return jax.shard_map(
        functools.partial(local, mesh.shape["ctx"], mesh.shape["head"]),
        mesh=mesh,
        in_specs=(
            P("ctx", "head"),
            P("ctx", "head"),
            P("ctx", "head"),
            P("ctx", "head"),
            P("head", None),
        ),
        out_specs=(P("ctx", "head"), P("ctx", "head"), P("ctx", "head")),
        check_vma=False,
    )
```

```python
import functools

import jax
import jax.numpy as jnp
from jax import lax
from jax.experimental import pallas as pl
from jax.experimental.pallas import tpu as pltpu
from jax.sharding import PartitionSpec as P

DH = 64
PAIR = 2 * DH
MESH = pl.DeviceIdType.MESH
NT = (((1,), (1,)), ((), ()))
NN = (((1,), (0,)), ((), ()))


def dot(a, b, dims):
    return lax.dot_general(a, b, dims, preferred_element_type=jnp.float32)


def inner_extent(n):
    best = 1
    while n % (2 * best) == 0 and (2 * best) ** 2 <= n:
        best *= 2
    return best


def kernel(Z, Y, X, C, kc, q_hbm, k_hbm, v_hbm, g_hbm, w_hbm, dq_ref, dk_ref, dv_ref,
           qbuf, q2buf, kvbuf, ktbuf, gbuf, wbuf, acc, dobuf, pbuf, dsbuf, part, s1, r1, s2, r2,
           loc_sem, w_sem, g_recv, gx_send, gc_send, gf_send, kv_recv, kvz_send, kvy_send, kvf_send,
           s1_send, r1_recv, s2_send, r2_recv):
    rows, width = q_hbm.shape
    r = k_hbm.shape[0]
    keys = Z * Y * r
    half = Z * r
    pairs = width // PAIR
    chunks = width // kc
    group = kc // PAIR
    groups = pairs // group
    c = lax.axis_index("ctx")
    h = lax.axis_index("head")
    z, y = c // Y, c % Y
    x, k = h // C, h % C

    def at_z(b):
        return {"ctx": lax.rem(z + b, Z) * Y + y, "head": h}

    def at_y(a):
        return {"ctx": z * Y + lax.rem(y + a, Y), "head": h}

    def at_x(d):
        return {"ctx": c, "head": lax.rem(x + d, X) * C + k}

    def at_core(d):
        return {"ctx": c, "head": x * C + lax.rem(k + d, C)}

    def remote(src, dst, send, recv, target):
        return pltpu.make_async_remote_copy(
            src_ref=src, dst_ref=dst, send_sem=send, recv_sem=recv,
            device_id=target, device_id_type=MESH)

    def slot(a, b):
        return pl.ds((a * Z + b) * r, r)

    kv_hbm = (k_hbm, v_hbm)

    loads = [
        pltpu.make_async_copy(g_hbm, gbuf.at[0, 0], loc_sem.at[0]),
        pltpu.make_async_copy(q_hbm, qbuf, loc_sem.at[1]),
        pltpu.make_async_copy(k_hbm, kvbuf.at[0, slot(0, 0)], loc_sem.at[2]),
        pltpu.make_async_copy(v_hbm, kvbuf.at[1, slot(0, 0)], loc_sem.at[3]),
    ]

    def w_load(d, e):
        block = lax.rem(x + d, X) * C + lax.rem(k + e, C)
        cols = pl.ds(pl.multiple_of(block * width, width), width)
        return pltpu.make_async_copy(w_hbm.at[:, cols], wbuf.at[d, e], w_sem.at[d, e])

    partners = ([at_z(b) for b in range(1, Z)] + [at_y(a) for a in range(1, Y)]
                + [at_x(d) for d in range(1, X)] + [at_core(d) for d in range(1, C)])
    barrier = pltpu.get_barrier_semaphore()
    for target in partners:
        pl.semaphore_signal(barrier, inc=1, device_id=target, device_id_type=MESH)
    loads[0].start()
    w_load(0, 0).start()
    pl.semaphore_wait(barrier, len(partners))

    def cols(j):
        return pl.ds(pl.multiple_of(j * kc, kc), kc)

    def gx(d, j):
        return remote(g_hbm.at[:, cols(j)], gbuf.at[X - d, 0, :, cols(j)],
                      gx_send.at[d, j], g_recv.at[X - d, 0, j], at_x(d))

    def gc(e):
        return remote(g_hbm, gbuf.at[0, C - e], gc_send.at[e], g_recv.at[0, C - e, 0], at_core(e))

    def gf(d, e, j):
        return remote(gbuf.at[d, 0, :, cols(j)], gbuf.at[d, C - e, :, cols(j)],
                      gf_send.at[d, e, j], g_recv.at[d, C - e, j], at_core(e))

    def kvz(t, b):
        return remote(kv_hbm[t], kvbuf.at[t, slot(0, Z - b)],
                      kvz_send.at[t, b], kv_recv.at[t, 0, Z - b], at_z(b))

    def kvy(t, a):
        return remote(kv_hbm[t], kvbuf.at[t, slot(Y - a, 0)],
                      kvy_send.at[t, a], kv_recv.at[t, Y - a, 0], at_y(a))

    def kvf(t, a, b):
        return remote(kvbuf.at[t, slot(0, b)], kvbuf.at[t, slot(Y - a, b)],
                      kvf_send.at[t, a, b], kv_recv.at[t, Y - a, b], at_y(a))

    def start_kv(t):
        for b in range(1, Z):
            kvz(t, Z - b).start()
        for a in range(1, Y):
            kvy(t, a).start()

    for d in range(1, X):
        gx(d, 0).start()
    start_kv(0)
    for e in range(1, C):
        gc(e).start()
    for j in range(1, chunks):
        for d in range(1, X):
            gx(d, j).start()
    for copy in loads[1:]:
        copy.start()
    for d in range(X):
        for e in range(C):
            if d + e:
                w_load(d, e).start()

    def forward_g(j):
        for d in range(1, X):
            gx(X - d, j).wait_recv()
            for e in range(1, C):
                gf(d, e, j).start()

    nearest = sorted(range(1, Z), key=lambda b: min(b, Z - b))

    def forward_kv(t):
        for i, b in enumerate(nearest):
            kvz(t, Z - b).wait_recv()
            for a in range(1, Y):
                kvf(t, a, b).start()
            if t == 0 and i == 0:
                start_kv(1)
        if t == 0 and not nearest:
            start_kv(1)

    def arrived_kv(t):
        for a in range(1, Y):
            kvy(t, Y - a).wait_recv()
            for b in range(1, Z):
                kvf(t, Y - a, b).wait_recv()

    def tiles(body):
        def step(n, carry):
            body(pl.ds(pl.multiple_of(n * kc, kc), kc))
            return carry

        lax.fori_loop(0, chunks, step, 0)

    def add_chunk(j):
        for d in range(1, X):
            for e in range(1, C):
                gf(d, C - e, j).wait_recv()

        def body(tile):
            total = acc[:, tile]
            for d in range(1, X):
                for e in range(C):
                    total += dot(gbuf[d, e, :, cols(j)], wbuf[d, e, tile, cols(j)], NT)
            acc[:, tile] = total

        tiles(body)

    loads[0].wait()
    for e in range(C):
        w_load(0, e).wait()
        if e:
            gc(C - e).wait_recv()

    def near_blocks(tile):
        total = dot(gbuf[0, 0], wbuf[0, 0, tile], NT)
        for e in range(1, C):
            total += dot(gbuf[0, e], wbuf[0, e, tile], NT)
        acc[:, tile] = total

    tiles(near_blocks)
    for d in range(1, X):
        for e in range(C):
            w_load(d, e).wait()

    lane = lax.broadcasted_iota(jnp.int32, (1, PAIR), 1)
    low = jnp.where(lane < DH, 1.0, 0.0).astype(jnp.bfloat16)
    high = jnp.where(lane < DH, 0.0, 1.0).astype(jnp.bfloat16)
    scale = DH ** -0.5

    def at_pair(p):
        return pl.ds(pl.multiple_of(p * PAIR, PAIR), PAIR)

    def both_heads(block):
        return jnp.concatenate((block * low, block * high), axis=0)

    def attention(g):
        members = [g * group + i for i in range(group)]
        queries = [both_heads(qbuf[:, at_pair(p)] * jnp.bfloat16(scale)) for p in members]
        key_pairs = [kvbuf[0, :, at_pair(p)] for p in members]
        scores = [dot(a, b, NT) for a, b in zip(key_pairs, queries)]
        exponents = [jnp.exp(s - jnp.max(s, axis=0, keepdims=True)) for s in scores]
        probs = [e * (1.0 / jnp.sum(e, axis=0, keepdims=True)) for e in exponents]
        for p, q2, key_pair, prob in zip(members, queries, key_pairs, probs):
            q2buf[p] = q2
            ktbuf[p] = key_pair.astype(jnp.float32).T.astype(jnp.bfloat16)
            pbuf[p] = prob

    loads[1].wait()
    loads[2].wait()
    forward_kv(0)
    arrived_kv(0)

    def gather_step(j, carry):
        forward_g(j)
        attention(j)

        @pl.when(j == min(1, chunks - 1))
        def _():
            forward_kv(1)

        add_chunk(j)
        return carry

    lax.fori_loop(0, chunks, gather_step, 0)
    dobuf[...] = acc[...].astype(jnp.bfloat16)
    loads[3].wait()
    arrived_kv(1)

    def send1(a, p):
        return remote(s1.at[a - 1, p], r1.at[Y - a - 1, p], s1_send.at[a - 1, p],
                      r1_recv.at[Y - a - 1, p], at_y(a))

    def send2(b, p):
        return remote(s2.at[b - 1, p], r2.at[Z - b - 1, p], s2_send.at[b - 1, p],
                      r2_recv.at[Z - b - 1, p], at_z(b))

    def terms(g):
        members = [g * group + i for i in range(group)]
        grads = [both_heads(dobuf[:, at_pair(p)]) for p in members]
        dps = [dot(kvbuf[1, :, at_pair(p)], do2, NT) for p, do2 in zip(members, grads)]
        probs = [pbuf[p] for p in members]
        lows = [prob.astype(jnp.bfloat16) for prob in probs]
        deltas = [jnp.sum(a.astype(jnp.float32) * b, axis=0, keepdims=True) for a, b in zip(lows, dps)]
        scored = [(a * (b - d)).astype(jnp.bfloat16) for a, b, d in zip(probs, dps, deltas)]
        value_terms = [dot(a, b, NN) for a, b in zip(lows, grads)]
        key_terms = [dot(ds, q2buf[p], NN) for ds, p in zip(scored, members)]
        for p, ds, key_term, value_term in zip(members, scored, key_terms, value_terms):
            dsbuf[p] = ds
            for t, term in enumerate((key_term, value_term)):
                part[p, t] = term[:half]
                for a in range(1, Y):
                    s1[a - 1, p, t] = term[a * half:(a + 1) * half].astype(jnp.bfloat16)
        for p in members:
            for a in range(1, Y):
                send1(a, p).start()

    def second(p):
        for a in range(1, Y):
            send1(Y - a, p).wait_recv()
        for t in range(2):
            total = part[p, t]
            for a in range(1, Y):
                total += r1[a - 1, p, t].astype(jnp.float32)
            part[p, t, :r] = total[:r]
            for b in range(1, Z):
                s2[b - 1, p, t] = total[b * r:(b + 1) * r].astype(jnp.bfloat16)
        for b in range(1, Z):
            send2(b, p).start()

    def query_part(p):
        dqt = dot(ktbuf[p], dsbuf[p], NN)
        both = jnp.concatenate((dqt[:DH, :rows], dqt[DH:, rows:]), axis=0)
        dq_ref[:, at_pair(p)] = (both.T * scale).astype(jnp.bfloat16)

    def relay(g):
        for i in range(group):
            second(g * group + i)

    def term_step(g, carry):
        terms(g)

        @pl.when(g >= 1)
        def _():
            relay(g - 1)
        return carry

    lax.fori_loop(0, groups, term_step, 0)

    def query_step(p, carry):
        query_part(p)

        @pl.when(p == pairs // 2 - 1 if pairs > 1 else p == 0)
        def _():
            relay(groups - 1)
        return carry

    lax.fori_loop(0, pairs, query_step, 0)

    def final_loop(p, carry):
        for b in range(1, Z):
            send2(Z - b, p).wait_recv()
        for t, out in enumerate((dk_ref, dv_ref)):
            total = part[p, t, :r]
            for b in range(1, Z):
                total += r2[b - 1, p, t].astype(jnp.float32)
            out[:, at_pair(p)] = total.astype(jnp.bfloat16)
        for a in range(1, Y):
            send1(a, p).wait_send()
        for b in range(1, Z):
            send2(b, p).wait_send()
        return carry

    lax.fori_loop(0, pairs, final_loop, 0)

    for j in range(chunks):
        for d in range(1, X):
            gx(d, j).wait_send()
            for e in range(1, C):
                gf(d, e, j).wait_send()
    for e in range(1, C):
        gc(e).wait_send()
    for t in range(2):
        for b in range(1, Z):
            kvz(t, b).wait_send()
            for a in range(1, Y):
                kvf(t, a, b).wait_send()
        for a in range(1, Y):
            kvy(t, a).wait_send()


def write_results(a, b, c, a_out, b_out, c_out, sem):
    copies = [pltpu.make_async_copy(src, dst, sem.at[i])
              for i, (src, dst) in enumerate(((a, a_out), (b, b_out), (c, c_out)))]
    for copy in copies:
        copy.start()
    for copy in copies:
        copy.wait()


def local(n, m, queries, enc_keys, enc_values, grad_out, out_weight):
    rows, width = queries.shape
    r = enc_keys.shape[0]
    Y = inner_extent(n)
    Z = n // Y
    C = 2 if m % 2 == 0 else 1
    X = m // C
    pairs = width // PAIR
    kc = PAIR * (2 if pairs % 2 == 0 else 1)
    chunks = width // kc
    keys, half = n * r, Z * r
    low, full = jnp.bfloat16, jnp.float32
    y1, z1 = max(Y - 1, 1), max(Z - 1, 1)
    dma = pltpu.SemaphoreType.DMA
    vmem = pltpu.VMEM
    results = pl.pallas_call(
        functools.partial(kernel, Z, Y, X, C, kc),
        out_shape=(
            pltpu.VMEM((rows, width), low),
            pltpu.VMEM((r, width), low),
            pltpu.VMEM((r, width), low),
        ),
        in_specs=[pl.BlockSpec(memory_space=pl.ANY)] * 5,
        out_specs=[pl.BlockSpec(memory_space=pltpu.VMEM)] * 3,
        scratch_shapes=[
            vmem((rows, width), low),
            vmem((pairs, 2 * rows, PAIR), low),
            vmem((2, keys, width), low),
            vmem((pairs, PAIR, keys), low),
            vmem((X, C, rows, width), low),
            vmem((X, C, width, width), low),
            vmem((rows, width), full),
            vmem((rows, width), low),
            vmem((pairs, keys, 2 * rows), full),
            vmem((pairs, keys, 2 * rows), low),
            vmem((pairs, 2, half, PAIR), full),
            vmem((y1, pairs, 2, half, PAIR), low),
            vmem((y1, pairs, 2, half, PAIR), low),
            vmem((z1, pairs, 2, r, PAIR), low),
            vmem((z1, pairs, 2, r, PAIR), low),
            dma((4,)),
            dma((X, C)),
            dma((X, C, chunks)),
            dma((X, chunks)),
            dma((C,)),
            dma((X, C, chunks)),
            dma((2, Y, Z)),
            dma((2, Z)),
            dma((2, Y)),
            dma((2, Y, Z)),
            dma((y1, pairs)),
            dma((y1, pairs)),
            dma((z1, pairs)),
            dma((z1, pairs)),
        ],
        compiler_params=pltpu.CompilerParams(
            collective_id=0, has_side_effects=True, vmem_limit_bytes=62 * 1024 * 1024),
    )(queries, enc_keys, enc_values, grad_out, out_weight)
    return pl.pallas_call(
        write_results,
        out_shape=tuple(jax.ShapeDtypeStruct(a.shape, a.dtype) for a in results),
        in_specs=[pl.BlockSpec(memory_space=pl.ANY)] * 3,
        out_specs=[pl.BlockSpec(memory_space=pl.ANY)] * 3,
        scratch_shapes=[dma((3,))],
    )(*results)


def solution(mesh):
    return jax.shard_map(
        functools.partial(local, mesh.shape["ctx"], mesh.shape["head"]),
        mesh=mesh,
        in_specs=(
            P("ctx", "head"),
            P("ctx", "head"),
            P("ctx", "head"),
            P("ctx", "head"),
            P("head", None),
        ),
        out_specs=(P("ctx", "head"), P("ctx", "head"), P("ctx", "head")),
        check_vma=False,
    )
```

```python
import functools

import jax
import jax.numpy as jnp
from jax import lax
from jax.experimental import pallas as pl
from jax.experimental.pallas import tpu as pltpu
from jax.sharding import PartitionSpec as P

DH = 64
PAIR = 2 * DH
MESH = pl.DeviceIdType.MESH
NT = (((1,), (1,)), ((), ()))
NN = (((1,), (0,)), ((), ()))


def dot(a, b, dims):
    return lax.dot_general(a, b, dims, preferred_element_type=jnp.float32)


def inner_extent(n):
    best = 1
    while n % (2 * best) == 0 and (2 * best) ** 2 <= n:
        best *= 2
    return best


def kernel(Z, Y, X, C, kc, q_hbm, k_hbm, v_hbm, g_hbm, w_hbm, dq_ref, dk_ref, dv_ref,
           qbuf, q2buf, kvbuf, ktbuf, gbuf, wbuf, acc, dobuf, pbuf, dsbuf, part, s1, r1, s2, r2,
           loc_sem, w_sem, g_recv, gx_send, gc_send, gf_send, kv_recv, kvz_send, kvy_send, kvf_send,
           s1_send, r1_recv, s2_send, r2_recv):
    rows, width = q_hbm.shape
    r = k_hbm.shape[0]
    keys = Z * Y * r
    half = Z * r
    pairs = width // PAIR
    chunks = width // kc
    group = 2 if pairs % 2 == 0 else 1
    groups = pairs // group
    c = lax.axis_index("ctx")
    h = lax.axis_index("head")
    z, y = c // Y, c % Y
    x, k = h // C, h % C

    def at_z(b):
        return {"ctx": lax.rem(z + b, Z) * Y + y, "head": h}

    def at_y(a):
        return {"ctx": z * Y + lax.rem(y + a, Y), "head": h}

    def at_x(d):
        return {"ctx": c, "head": lax.rem(x + d, X) * C + k}

    def at_core(d):
        return {"ctx": c, "head": x * C + lax.rem(k + d, C)}

    def remote(src, dst, send, recv, target):
        return pltpu.make_async_remote_copy(
            src_ref=src, dst_ref=dst, send_sem=send, recv_sem=recv,
            device_id=target, device_id_type=MESH)

    def slot(a, b):
        return pl.ds((a * Z + b) * r, r)

    loads = [
        pltpu.make_async_copy(g_hbm, gbuf.at[0, 0], loc_sem.at[0]),
        pltpu.make_async_copy(q_hbm, qbuf, loc_sem.at[1]),
        pltpu.make_async_copy(k_hbm, kvbuf.at[0, slot(0, 0)], loc_sem.at[2]),
        pltpu.make_async_copy(v_hbm, kvbuf.at[1, slot(0, 0)], loc_sem.at[3]),
    ]

    def w_load(d, e):
        block = lax.rem(x + d, X) * C + lax.rem(k + e, C)
        cols = pl.ds(pl.multiple_of(block * width, width), width)
        return pltpu.make_async_copy(w_hbm.at[:, cols], wbuf.at[d, e], w_sem.at[d, e])

    partners = ([at_z(b) for b in range(1, Z)] + [at_y(a) for a in range(1, Y)]
                + [at_x(d) for d in range(1, X)] + [at_core(d) for d in range(1, C)])
    barrier = pltpu.get_barrier_semaphore()
    for target in partners:
        pl.semaphore_signal(barrier, inc=1, device_id=target, device_id_type=MESH)
    for i in (0, 2, 3):
        loads[i].start()
    w_load(0, 0).start()
    pl.semaphore_wait(barrier, len(partners))

    def cols(j):
        return pl.ds(j * kc, kc)

    def gx(d, j):
        return remote(gbuf.at[0, 0, :, cols(j)], gbuf.at[X - d, 0, :, cols(j)],
                      gx_send.at[d, j], g_recv.at[X - d, 0, j], at_x(d))

    def gc(e):
        return remote(gbuf.at[0, 0], gbuf.at[0, C - e], gc_send.at[e], g_recv.at[0, C - e, 0], at_core(e))

    def gf(d, e, j):
        return remote(gbuf.at[d, 0, :, cols(j)], gbuf.at[d, C - e, :, cols(j)],
                      gf_send.at[d, e, j], g_recv.at[d, C - e, j], at_core(e))

    def kvz(t, b):
        return remote(kvbuf.at[t, slot(0, 0)], kvbuf.at[t, slot(0, Z - b)],
                      kvz_send.at[t, b], kv_recv.at[t, 0, Z - b], at_z(b))

    def kvy(t, a):
        return remote(kvbuf.at[t, slot(0, 0)], kvbuf.at[t, slot(Y - a, 0)],
                      kvy_send.at[t, a], kv_recv.at[t, Y - a, 0], at_y(a))

    def kvf(t, a, b):
        return remote(kvbuf.at[t, slot(0, b)], kvbuf.at[t, slot(Y - a, b)],
                      kvf_send.at[t, a, b], kv_recv.at[t, Y - a, b], at_y(a))

    def start_kv(t):
        for b in range(1, Z):
            kvz(t, Z - b).start()
        for a in range(1, Y):
            kvy(t, a).start()

    loads[0].wait()
    for d in range(1, X):
        gx(d, 0).start()
    loads[2].wait()
    start_kv(0)
    for e in range(1, C):
        gc(e).start()
    for j in range(1, chunks):
        for d in range(1, X):
            gx(d, j).start()
    loads[3].wait()
    loads[1].start()
    for d in range(X):
        for e in range(C):
            if d + e:
                w_load(d, e).start()

    def forward_g(j):
        for d in range(1, X):
            gx(X - d, j).wait_recv()
            for e in range(1, C):
                gf(d, e, j).start()

    nearest = sorted(range(1, Z), key=lambda b: min(b, Z - b))

    def forward_kv(t):
        for i, b in enumerate(nearest):
            kvz(t, Z - b).wait_recv()
            for a in range(1, Y):
                kvf(t, a, b).start()
            if t == 0 and i == 0:
                start_kv(1)
        if t == 0 and not nearest:
            start_kv(1)

    def arrived_kv(t):
        for a in range(1, Y):
            kvy(t, Y - a).wait_recv()
            for b in range(1, Z):
                kvf(t, Y - a, b).wait_recv()

    def add_chunks(first, last):
        span = slice(first * kc, last * kc)
        total = acc[...]
        for d in range(1, X):
            for e in range(C):
                if e:
                    for j in range(first, last):
                        gf(d, C - e, j).wait_recv()
                total += dot(wbuf[d, e, :, span], gbuf[d, e, :, span], NT)
        acc[...] = total

    def near_blocks():
        w_load(0, 0).wait()
        total = dot(wbuf[0, 0], gbuf[0, 0], NT)
        for e in range(1, C):
            gc(C - e).wait_recv()
            w_load(0, e).wait()
            total += dot(wbuf[0, e], gbuf[0, e], NT)
        acc[...] = total
        for d in range(1, X):
            for e in range(C):
                w_load(d, e).wait()

    lane = lax.broadcasted_iota(jnp.int32, (1, PAIR), 1)
    low = jnp.where(lane < DH, 1.0, 0.0).astype(jnp.bfloat16)
    high = jnp.where(lane < DH, 0.0, 1.0).astype(jnp.bfloat16)
    scale = DH ** -0.5
    row = lax.broadcasted_iota(jnp.int32, (PAIR, 1), 0)
    upper = jnp.where(row < DH, 1.0, 0.0).astype(jnp.bfloat16)
    lower = jnp.where(row < DH, 0.0, 1.0).astype(jnp.bfloat16)

    def at_pair(p):
        return pl.ds(pl.multiple_of(p * PAIR, PAIR), PAIR)

    def both_heads(block):
        return jnp.concatenate((block * low, block * high), axis=0)

    def attention(g, carry):
        members = [g * group + i for i in range(group)]
        queries = [both_heads(qbuf[:, at_pair(p)] * jnp.bfloat16(scale)) for p in members]
        key_pairs = [kvbuf[0, :, at_pair(p)] for p in members]
        scores = [dot(a, b, NT) for a, b in zip(key_pairs, queries)]
        exponents = [jnp.exp(s - jnp.max(s, axis=0, keepdims=True)) for s in scores]
        probs = [e * (1.0 / jnp.sum(e, axis=0, keepdims=True)) for e in exponents]
        for p, q2, key_pair, prob in zip(members, queries, key_pairs, probs):
            q2buf[p] = q2
            ktbuf[p] = key_pair.astype(jnp.float32).T.astype(jnp.bfloat16)
            pbuf[p] = prob
        return carry

    def attend(first, last):
        if first < last:
            lax.fori_loop(first, last, attention, 0)

    forward_kv(0)
    forward_g(0)
    near_blocks()
    if chunks > 1:
        forward_g(1)
    loads[1].wait()
    arrived_kv(0)
    attend(0, groups // 4)
    if chunks > 2:
        forward_g(2)
    attend(groups // 4, groups // 2)
    forward_kv(1)
    for j in range(3, chunks):
        forward_g(j)
    add_chunks(0, (chunks + 1) // 2)
    attend(groups // 2, groups)
    if chunks > 1:
        add_chunks((chunks + 1) // 2, chunks)
    dobuf[...] = acc[...].astype(jnp.bfloat16)
    arrived_kv(1)

    def send1(a, p):
        return remote(s1.at[a - 1, p], r1.at[Y - a - 1, p], s1_send.at[a - 1],
                      r1_recv.at[Y - a - 1, p], at_y(a))

    def send2(b, p):
        return remote(s2.at[b - 1, p], r2.at[Z - b - 1, p], s2_send.at[b - 1],
                      r2_recv.at[Z - b - 1], at_z(b))

    def terms(g):
        members = [g * group + i for i in range(group)]
        blocks = [dobuf[at_pair(p)] for p in members]
        grads = [jnp.concatenate((block * upper, block * lower), axis=1) for block in blocks]
        dps = [dot(kvbuf[1, :, at_pair(p)], do2, NN) for p, do2 in zip(members, grads)]
        probs = [pbuf[p] for p in members]
        lows = [prob.astype(jnp.bfloat16) for prob in probs]
        deltas = [jnp.sum(a.astype(jnp.float32) * b, axis=0, keepdims=True) for a, b in zip(lows, dps)]
        scored = [(a * (b - d)).astype(jnp.bfloat16) for a, b, d in zip(probs, dps, deltas)]
        value_terms = [dot(a, b, NT) for a, b in zip(lows, grads)]
        key_terms = [dot(ds, q2buf[p], NN) for ds, p in zip(scored, members)]
        for p, ds, key_term, value_term in zip(members, scored, key_terms, value_terms):
            dsbuf[p] = ds
            for t, term in enumerate((key_term, value_term)):
                part[p, t] = term[:half]
                for a in range(1, Y):
                    s1[a - 1, p, t] = term[a * half:(a + 1) * half].astype(jnp.bfloat16)
        for p in members:
            for a in range(1, Y):
                send1(a, p).start()

    def second(p):
        for a in range(1, Y):
            send1(Y - a, p).wait_recv()
        for t in range(2):
            total = part[p, t]
            for a in range(1, Y):
                total += r1[a - 1, p, t].astype(jnp.float32)
            part[p, t, :r] = total[:r]
            for b in range(1, Z):
                s2[b - 1, p, t] = total[b * r:(b + 1) * r].astype(jnp.bfloat16)
        for b in range(1, Z):
            send2(b, p).start()

    def query_part(p):
        dqt = dot(ktbuf[p], dsbuf[p], NN)
        both = jnp.concatenate((dqt[:DH, :rows], dqt[DH:, rows:]), axis=0)
        dq_ref[:, at_pair(p)] = (both.T * scale).astype(jnp.bfloat16)

    def relay(g):
        for i in range(group):
            query_part(g * group + i)
            second(g * group + i)

    def first_loop(g, carry):
        terms(g)

        @pl.when(g >= 1)
        def _():
            relay(g - 1)
        return carry

    lax.fori_loop(0, groups, first_loop, 0)
    relay(groups - 1)

    def all1(a):
        return remote(s1.at[a - 1], r1.at[Y - a - 1], s1_send.at[a - 1], r1_recv.at[Y - a - 1, 0], at_y(a))

    def all2(b):
        return remote(s2.at[b - 1], r2.at[Z - b - 1], s2_send.at[b - 1], r2_recv.at[Z - b - 1], at_z(b))

    for b in range(1, Z):
        all2(Z - b).wait_recv()

    for p in range(pairs):
        for t, out in enumerate((dk_ref, dv_ref)):
            total = part[p, t, :r]
            for b in range(1, Z):
                total += r2[b - 1, p, t].astype(jnp.float32)
            out[:, p * PAIR:(p + 1) * PAIR] = total.astype(jnp.bfloat16)
    for a in range(1, Y):
        all1(a).wait_send()
    for b in range(1, Z):
        all2(b).wait_send()

    for j in range(chunks):
        for d in range(1, X):
            gx(d, j).wait_send()
            for e in range(1, C):
                gf(d, e, j).wait_send()
    for e in range(1, C):
        gc(e).wait_send()
    for t in range(2):
        for b in range(1, Z):
            kvz(t, b).wait_send()
            for a in range(1, Y):
                kvf(t, a, b).wait_send()
        for a in range(1, Y):
            kvy(t, a).wait_send()


def local(n, m, queries, enc_keys, enc_values, grad_out, out_weight):
    rows, width = queries.shape
    r = enc_keys.shape[0]
    Y = inner_extent(n)
    Z = n // Y
    C = 2 if m % 2 == 0 else 1
    X = m // C
    kc = min(256, width)
    pairs = width // PAIR
    chunks = width // kc
    keys, half = n * r, Z * r
    low, full = jnp.bfloat16, jnp.float32
    y1, z1 = max(Y - 1, 1), max(Z - 1, 1)
    dma = pltpu.SemaphoreType.DMA
    vmem = pltpu.VMEM
    return pl.pallas_call(
        functools.partial(kernel, Z, Y, X, C, kc),
        out_shape=(
            pltpu.VMEM((rows, width), low),
            pltpu.VMEM((r, width), low),
            pltpu.VMEM((r, width), low),
        ),
        in_specs=[pl.BlockSpec(memory_space=pl.ANY)] * 5,
        out_specs=[pl.BlockSpec(memory_space=pltpu.VMEM)] * 3,
        scratch_shapes=[
            vmem((rows, width), low),
            vmem((pairs, 2 * rows, PAIR), low),
            vmem((2, keys, width), low),
            vmem((pairs, PAIR, keys), low),
            vmem((X, C, rows, width), low),
            vmem((X, C, width, width), low),
            vmem((width, rows), full),
            vmem((width, rows), low),
            vmem((pairs, keys, 2 * rows), full),
            vmem((pairs, keys, 2 * rows), low),
            vmem((pairs, 2, half, PAIR), full),
            vmem((y1, pairs, 2, half, PAIR), low),
            vmem((y1, pairs, 2, half, PAIR), low),
            vmem((z1, pairs, 2, r, PAIR), low),
            vmem((z1, pairs, 2, r, PAIR), low),
            dma((4,)),
            dma((X, C)),
            dma((X, C, chunks)),
            dma((X, chunks)),
            dma((C,)),
            dma((X, C, chunks)),
            dma((2, Y, Z)),
            dma((2, Z)),
            dma((2, Y)),
            dma((2, Y, Z)),
            dma((y1,)),
            dma((y1, pairs)),
            dma((z1,)),
            dma((z1,)),
        ],
        compiler_params=pltpu.CompilerParams(
            collective_id=0, has_side_effects=True, vmem_limit_bytes=62 * 1024 * 1024),
    )(queries, enc_keys, enc_values, grad_out, out_weight)


def solution(mesh):
    return jax.shard_map(
        functools.partial(local, mesh.shape["ctx"], mesh.shape["head"]),
        mesh=mesh,
        in_specs=(
            P("ctx", "head"),
            P("ctx", "head"),
            P("ctx", "head"),
            P("ctx", "head"),
            P("head", None),
        ),
        out_specs=(P("ctx", "head"), P("ctx", "head"), P("ctx", "head")),
        check_vma=False,
    )
```

```python
import functools

import jax
import jax.numpy as jnp
from jax import lax
from jax.experimental import pallas as pl
from jax.experimental.pallas import tpu as pltpu
from jax.sharding import PartitionSpec as P

DH = 64
PAIR = 2 * DH
MESH = pl.DeviceIdType.MESH
NT = (((1,), (1,)), ((), ()))
NN = (((1,), (0,)), ((), ()))


def dot(a, b, dims):
    return lax.dot_general(a, b, dims, preferred_element_type=jnp.float32)


def inner_extent(n):
    best = 1
    while n % (2 * best) == 0 and (2 * best) ** 2 <= n:
        best *= 2
    return best


def kernel(Z, Y, X, C, kc, q_hbm, k_hbm, v_hbm, g_hbm, w_hbm, dq_ref, dk_ref, dv_ref,
           qbuf, q2buf, kvbuf, ktbuf, gbuf, wbuf, acc, dobuf, pbuf, dsbuf, part, s1, r1, s2, r2,
           loc_sem, w_sem, g_recv, gx_send, gc_send, gf_send, kv_recv, kvz_send, kvy_send, kvf_send,
           s1_send, r1_recv, s2_send, r2_recv):
    rows, width = q_hbm.shape
    r = k_hbm.shape[0]
    keys = Z * Y * r
    half = Z * r
    pairs = width // PAIR
    chunks = width // kc
    group = 2 if pairs % 2 == 0 else 1
    groups = pairs // group
    c = lax.axis_index("ctx")
    h = lax.axis_index("head")
    z, y = c // Y, c % Y
    x, k = h // C, h % C

    def at_z(b):
        return {"ctx": lax.rem(z + b, Z) * Y + y, "head": h}

    def at_y(a):
        return {"ctx": z * Y + lax.rem(y + a, Y), "head": h}

    def at_x(d):
        return {"ctx": c, "head": lax.rem(x + d, X) * C + k}

    def at_core(d):
        return {"ctx": c, "head": x * C + lax.rem(k + d, C)}

    def remote(src, dst, send, recv, target):
        return pltpu.make_async_remote_copy(
            src_ref=src, dst_ref=dst, send_sem=send, recv_sem=recv,
            device_id=target, device_id_type=MESH)

    def slot(a, b):
        return pl.ds((a * Z + b) * r, r)

    loads = [
        pltpu.make_async_copy(g_hbm, gbuf.at[0, 0], loc_sem.at[0]),
        pltpu.make_async_copy(q_hbm, qbuf, loc_sem.at[1]),
        pltpu.make_async_copy(k_hbm, kvbuf.at[0, slot(0, 0)], loc_sem.at[2]),
        pltpu.make_async_copy(v_hbm, kvbuf.at[1, slot(0, 0)], loc_sem.at[3]),
    ]

    def w_load(d, e):
        block = lax.rem(x + d, X) * C + lax.rem(k + e, C)
        cols = pl.ds(pl.multiple_of(block * width, width), width)
        return pltpu.make_async_copy(w_hbm.at[:, cols], wbuf.at[d, e], w_sem.at[d, e])

    partners = ([at_z(b) for b in range(1, Z)] + [at_y(a) for a in range(1, Y)]
                + [at_x(d) for d in range(1, X)] + [at_core(d) for d in range(1, C)])
    barrier = pltpu.get_barrier_semaphore()
    for target in partners:
        pl.semaphore_signal(barrier, inc=1, device_id=target, device_id_type=MESH)
    for i in (0, 2, 3):
        loads[i].start()
    w_load(0, 0).start()
    pl.semaphore_wait(barrier, len(partners))

    def cols(j):
        return pl.ds(j * kc, kc)

    def gx(d, j):
        return remote(gbuf.at[0, 0, :, cols(j)], gbuf.at[X - d, 0, :, cols(j)],
                      gx_send.at[d, j], g_recv.at[X - d, 0, j], at_x(d))

    def gc(e):
        return remote(gbuf.at[0, 0], gbuf.at[0, C - e], gc_send.at[e], g_recv.at[0, C - e, 0], at_core(e))

    def gf(d, e, j):
        return remote(gbuf.at[d, 0, :, cols(j)], gbuf.at[d, C - e, :, cols(j)],
                      gf_send.at[d, e, j], g_recv.at[d, C - e, j], at_core(e))

    def kv_up(t, i):
        return remote(kvbuf.at[t, slot(0, (Z - i) % Z)], kvbuf.at[t, slot(0, Z - i - 1)],
                      kvz_send.at[t, 0, i], kv_recv.at[t, 0, Z - i - 1], at_z(1))

    def kv_down(t, i):
        return remote(kvbuf.at[t, slot(0, i)], kvbuf.at[t, slot(0, i + 1)],
                      kvz_send.at[t, 1, i], kv_recv.at[t, 0, i + 1], at_z(Z - 1))

    def goes_up(i):
        return jnp.logical_and(z >= i, z < Z - 1)

    def goes_down(i):
        return jnp.logical_and(z + i <= Z - 1, z > 0)

    def kvy(t, a):
        return remote(kvbuf.at[t, slot(0, 0)], kvbuf.at[t, slot(Y - a, 0)],
                      kvy_send.at[t, a], kv_recv.at[t, Y - a, 0], at_y(a))

    def kvf(t, a, b):
        return remote(kvbuf.at[t, slot(0, b)], kvbuf.at[t, slot(Y - a, b)],
                      kvf_send.at[t, a, b], kv_recv.at[t, Y - a, b], at_y(a))

    def start_kv(t):
        if Z > 1:
            pl.when(goes_up(0))(lambda: kv_up(t, 0).start())
            pl.when(goes_down(0))(lambda: kv_down(t, 0).start())
        for a in range(1, Y):
            kvy(t, a).start()

    loads[0].wait()
    for d in range(1, X):
        gx(d, 0).start()
    loads[2].wait()
    start_kv(0)
    loads[3].wait()
    start_kv(1)
    for e in range(1, C):
        gc(e).start()
    for j in range(1, chunks):
        for d in range(1, X):
            gx(d, j).start()
    loads[1].start()
    for d in range(X):
        for e in range(C):
            if d + e:
                w_load(d, e).start()

    def forward_g(j):
        for d in range(1, X):
            gx(X - d, j).wait_recv()
            for e in range(1, C):
                gf(d, e, j).start()

    def relay_kv(t, i):
        if i > Z - 1:
            return

        @pl.when(z >= i)
        def _():
            kv_up(t, i - 1).wait_recv()
            if i < Z - 1:
                pl.when(z < Z - 1)(lambda: kv_up(t, i).start())
            for a in range(1, Y):
                kvf(t, a, Z - i).start()

        @pl.when(z + i <= Z - 1)
        def _():
            kv_down(t, i - 1).wait_recv()
            if i < Z - 1:
                pl.when(z > 0)(lambda: kv_down(t, i).start())
            for a in range(1, Y):
                kvf(t, a, i).start()

    def arrived_kv(t):
        for a in range(1, Y):
            kvy(t, Y - a).wait_recv()
            for b in range(1, Z):
                kvf(t, Y - a, b).wait_recv()

    def add_chunks(first, last):
        span = slice(first * kc, last * kc)
        total = acc[...]
        for d in range(1, X):
            for e in range(C):
                if e:
                    for j in range(first, last):
                        gf(d, C - e, j).wait_recv()
                total += dot(wbuf[d, e, :, span], gbuf[d, e, :, span], NT)
        acc[...] = total

    def own_block():
        w_load(0, 0).wait()
        acc[...] = dot(wbuf[0, 0], gbuf[0, 0], NT)

    def core_blocks():
        for e in range(1, C):
            gc(C - e).wait_recv()
            w_load(0, e).wait()
            acc[...] += dot(wbuf[0, e], gbuf[0, e], NT)
        for d in range(1, X):
            for e in range(C):
                w_load(d, e).wait()

    lane = lax.broadcasted_iota(jnp.int32, (1, PAIR), 1)
    low = jnp.where(lane < DH, 1.0, 0.0).astype(jnp.bfloat16)
    high = jnp.where(lane < DH, 0.0, 1.0).astype(jnp.bfloat16)
    scale = DH ** -0.5
    row = lax.broadcasted_iota(jnp.int32, (PAIR, 1), 0)
    upper = jnp.where(row < DH, 1.0, 0.0).astype(jnp.bfloat16)
    lower = jnp.where(row < DH, 0.0, 1.0).astype(jnp.bfloat16)

    def at_pair(p):
        return pl.ds(pl.multiple_of(p * PAIR, PAIR), PAIR)

    def both_heads(block):
        return jnp.concatenate((block * low, block * high), axis=0)

    def attention(g, carry):
        members = [g * group + i for i in range(group)]
        queries = [both_heads(qbuf[:, at_pair(p)] * jnp.bfloat16(scale)) for p in members]
        key_pairs = [kvbuf[0, :, at_pair(p)] for p in members]
        scores = [dot(a, b, NT) for a, b in zip(key_pairs, queries)]
        exponents = [jnp.exp(s - jnp.max(s, axis=0, keepdims=True)) for s in scores]
        probs = [e * (1.0 / jnp.sum(e, axis=0, keepdims=True)) for e in exponents]
        for p, q2, key_pair, prob in zip(members, queries, key_pairs, probs):
            q2buf[p] = q2
            ktbuf[p] = key_pair.astype(jnp.float32).T.astype(jnp.bfloat16)
            pbuf[p] = prob
        return carry

    def attend(first, last):
        if first < last:
            lax.fori_loop(first, last, attention, 0)

    mid = (chunks + 1) // 2
    own_block()
    relay_kv(0, 1)
    relay_kv(1, 1)
    core_blocks()
    relay_kv(0, 2)
    forward_g(0)
    relay_kv(1, 2)
    for i in range(3, Z):
        relay_kv(0, i)
    for j in range(1, mid):
        forward_g(j)
    add_chunks(0, mid)
    for i in range(3, Z):
        relay_kv(1, i)
    loads[1].wait()
    arrived_kv(0)
    attend(0, groups // 2)
    for j in range(mid, chunks - 1):
        forward_g(j)
    attend(groups // 2, groups)
    if chunks > 1:
        forward_g(chunks - 1)
        if mid < chunks - 1:
            add_chunks(mid, chunks - 1)
        add_chunks(chunks - 1, chunks)
    dobuf[...] = acc[...].astype(jnp.bfloat16)
    arrived_kv(1)

    def send1(a, p):
        return remote(s1.at[a - 1, p], r1.at[Y - a - 1, p], s1_send.at[a - 1],
                      r1_recv.at[Y - a - 1, p], at_y(a))

    def send2(b, p):
        return remote(s2.at[b - 1, p], r2.at[Z - b - 1, p], s2_send.at[b - 1],
                      r2_recv.at[Z - b - 1], at_z(b))

    def terms(g):
        members = [g * group + i for i in range(group)]
        blocks = [dobuf[at_pair(p)] for p in members]
        grads = [jnp.concatenate((block * upper, block * lower), axis=1) for block in blocks]
        dps = [dot(kvbuf[1, :, at_pair(p)], do2, NN) for p, do2 in zip(members, grads)]
        probs = [pbuf[p] for p in members]
        lows = [prob.astype(jnp.bfloat16) for prob in probs]
        deltas = [jnp.sum(a.astype(jnp.float32) * b, axis=0, keepdims=True) for a, b in zip(lows, dps)]
        scored = [(a * (b - d)).astype(jnp.bfloat16) for a, b, d in zip(probs, dps, deltas)]
        value_terms = [dot(a, b, NT) for a, b in zip(lows, grads)]
        key_terms = [dot(ds, q2buf[p], NN) for ds, p in zip(scored, members)]
        for p, ds, key_term, value_term in zip(members, scored, key_terms, value_terms):
            dsbuf[p] = ds
            for t, term in enumerate((key_term, value_term)):
                part[p, t] = term[:half]
                for a in range(1, Y):
                    s1[a - 1, p, t] = term[a * half:(a + 1) * half].astype(jnp.bfloat16)
        for p in members:
            for a in range(1, Y):
                send1(a, p).start()

    def second(p):
        for a in range(1, Y):
            send1(Y - a, p).wait_recv()
        for t in range(2):
            total = part[p, t]
            for a in range(1, Y):
                total += r1[a - 1, p, t].astype(jnp.float32)
            part[p, t, :r] = total[:r]
            for b in range(1, Z):
                s2[b - 1, p, t] = total[b * r:(b + 1) * r].astype(jnp.bfloat16)
        for b in range(1, Z):
            send2(b, p).start()

    def query_part(p):
        dqt = dot(ktbuf[p], dsbuf[p], NN)
        both = jnp.concatenate((dqt[:DH, :rows], dqt[DH:, rows:]), axis=0)
        dq_ref[:, at_pair(p)] = (both.T * scale).astype(jnp.bfloat16)

    def relay(g):
        for i in range(group):
            query_part(g * group + i)
            second(g * group + i)

    def first_loop(g, carry):
        terms(g)

        @pl.when(g >= 1)
        def _():
            relay(g - 1)
        return carry

    lax.fori_loop(0, groups, first_loop, 0)
    relay(groups - 1)

    def all1(a):
        return remote(s1.at[a - 1], r1.at[Y - a - 1], s1_send.at[a - 1], r1_recv.at[Y - a - 1, 0], at_y(a))

    def all2(b):
        return remote(s2.at[b - 1], r2.at[Z - b - 1], s2_send.at[b - 1], r2_recv.at[Z - b - 1], at_z(b))

    for b in range(1, Z):
        all2(Z - b).wait_recv()

    for p in range(pairs):
        for t, out in enumerate((dk_ref, dv_ref)):
            total = part[p, t, :r]
            for b in range(1, Z):
                total += r2[b - 1, p, t].astype(jnp.float32)
            out[:, p * PAIR:(p + 1) * PAIR] = total.astype(jnp.bfloat16)
    for a in range(1, Y):
        all1(a).wait_send()
    for b in range(1, Z):
        all2(b).wait_send()

    for j in range(chunks):
        for d in range(1, X):
            gx(d, j).wait_send()
            for e in range(1, C):
                gf(d, e, j).wait_send()
    for e in range(1, C):
        gc(e).wait_send()
    for t in range(2):
        for i in range(Z - 1):
            pl.when(goes_up(i))(lambda: kv_up(t, i).wait_send())
            pl.when(goes_down(i))(lambda: kv_down(t, i).wait_send())
        for b in range(1, Z):
            for a in range(1, Y):
                kvf(t, a, b).wait_send()
        for a in range(1, Y):
            kvy(t, a).wait_send()


def local(n, m, queries, enc_keys, enc_values, grad_out, out_weight):
    rows, width = queries.shape
    r = enc_keys.shape[0]
    Y = inner_extent(n)
    Z = n // Y
    C = 2 if m % 2 == 0 else 1
    X = m // C
    kc = min(256, width)
    pairs = width // PAIR
    chunks = width // kc
    keys, half = n * r, Z * r
    low, full = jnp.bfloat16, jnp.float32
    y1, z1 = max(Y - 1, 1), max(Z - 1, 1)
    dma = pltpu.SemaphoreType.DMA
    vmem = pltpu.VMEM
    return pl.pallas_call(
        functools.partial(kernel, Z, Y, X, C, kc),
        out_shape=(
            pltpu.VMEM((rows, width), low),
            pltpu.VMEM((r, width), low),
            pltpu.VMEM((r, width), low),
        ),
        in_specs=[pl.BlockSpec(memory_space=pl.ANY)] * 5,
        out_specs=[pl.BlockSpec(memory_space=pltpu.VMEM)] * 3,
        scratch_shapes=[
            vmem((rows, width), low),
            vmem((pairs, 2 * rows, PAIR), low),
            vmem((2, keys, width), low),
            vmem((pairs, PAIR, keys), low),
            vmem((X, C, rows, width), low),
            vmem((X, C, width, width), low),
            vmem((width, rows), full),
            vmem((width, rows), low),
            vmem((pairs, keys, 2 * rows), full),
            vmem((pairs, keys, 2 * rows), low),
            vmem((pairs, 2, half, PAIR), full),
            vmem((y1, pairs, 2, half, PAIR), low),
            vmem((y1, pairs, 2, half, PAIR), low),
            vmem((z1, pairs, 2, r, PAIR), low),
            vmem((z1, pairs, 2, r, PAIR), low),
            dma((4,)),
            dma((X, C)),
            dma((X, C, chunks)),
            dma((X, chunks)),
            dma((C,)),
            dma((X, C, chunks)),
            dma((2, Y, Z)),
            dma((2, 2, Z)),
            dma((2, Y)),
            dma((2, Y, Z)),
            dma((y1,)),
            dma((y1, pairs)),
            dma((z1,)),
            dma((z1,)),
        ],
        compiler_params=pltpu.CompilerParams(
            collective_id=0, has_side_effects=True, vmem_limit_bytes=62 * 1024 * 1024),
    )(queries, enc_keys, enc_values, grad_out, out_weight)


def solution(mesh):
    return jax.shard_map(
        functools.partial(local, mesh.shape["ctx"], mesh.shape["head"]),
        mesh=mesh,
        in_specs=(
            P("ctx", "head"),
            P("ctx", "head"),
            P("ctx", "head"),
            P("ctx", "head"),
            P("head", None),
        ),
        out_specs=(P("ctx", "head"), P("ctx", "head"), P("ctx", "head")),
        check_vma=False,
    )
```

```python
import functools

import jax
import jax.numpy as jnp
from jax import lax
from jax.experimental import pallas as pl
from jax.experimental.pallas import tpu as pltpu
from jax.sharding import PartitionSpec as P

DH = 64
PAIR = 2 * DH
MESH = pl.DeviceIdType.MESH
NT = (((1,), (1,)), ((), ()))
NN = (((1,), (0,)), ((), ()))


def dot(a, b, dims):
    return lax.dot_general(a, b, dims, preferred_element_type=jnp.float32)


def inner_extent(n):
    best = 1
    while n % (2 * best) == 0 and (2 * best) ** 2 <= n:
        best *= 2
    return best


def kernel(Z, Y, X, C, kc, q_hbm, k_hbm, v_hbm, g_hbm, w_hbm, dq_ref, dk_ref, dv_ref,
           qbuf, q2buf, kvbuf, ktbuf, gbuf, wbuf, acc, pbuf, dsbuf, part, s1, r1, s2, r2,
           loc_sem, w_sem, g_recv, gx_send, gc_send, gf_send, kv_recv, kvz_send, kvy_send, kvf_send,
           s1_send, r1_recv, s2_send, r2_recv):
    rows, width = q_hbm.shape
    r = k_hbm.shape[0]
    keys = Z * Y * r
    half = Z * r
    pairs = width // PAIR
    chunks = width // kc
    group = 2 if pairs % 2 == 0 else 1
    groups = pairs // group
    c = lax.axis_index("ctx")
    h = lax.axis_index("head")
    z, y = c // Y, c % Y
    x, k = h // C, h % C

    def at_z(b):
        return {"ctx": lax.rem(z + b, Z) * Y + y, "head": h}

    def at_y(a):
        return {"ctx": z * Y + lax.rem(y + a, Y), "head": h}

    def at_x(d):
        return {"ctx": c, "head": lax.rem(x + d, X) * C + k}

    def at_core(d):
        return {"ctx": c, "head": x * C + lax.rem(k + d, C)}

    def remote(src, dst, send, recv, target):
        return pltpu.make_async_remote_copy(
            src_ref=src, dst_ref=dst, send_sem=send, recv_sem=recv,
            device_id=target, device_id_type=MESH)

    def slot(a, b):
        return pl.ds((a * Z + b) * r, r)

    loads = [
        pltpu.make_async_copy(g_hbm, gbuf.at[0, 0], loc_sem.at[0]),
        pltpu.make_async_copy(q_hbm, qbuf, loc_sem.at[1]),
        pltpu.make_async_copy(k_hbm, kvbuf.at[0, slot(0, 0)], loc_sem.at[2]),
        pltpu.make_async_copy(v_hbm, kvbuf.at[1, slot(0, 0)], loc_sem.at[3]),
    ]

    def w_load(d, e):
        block = lax.rem(x + d, X) * C + lax.rem(k + e, C)
        cols = pl.ds(pl.multiple_of(block * width, width), width)
        return pltpu.make_async_copy(w_hbm.at[:, cols], wbuf.at[d, e], w_sem.at[d, e])

    partners = ([at_z(b) for b in range(1, Z)] + [at_y(a) for a in range(1, Y)]
                + [at_x(d) for d in range(1, X)] + [at_core(d) for d in range(1, C)])
    barrier = pltpu.get_barrier_semaphore()
    for target in partners:
        pl.semaphore_signal(barrier, inc=1, device_id=target, device_id_type=MESH)
    for i in (0, 2, 3):
        loads[i].start()
    w_load(0, 0).start()
    pl.semaphore_wait(barrier, len(partners))

    def cols(j):
        return pl.ds(j * kc, kc)

    def gx(d, j):
        return remote(gbuf.at[0, 0, :, cols(j)], gbuf.at[X - d, 0, :, cols(j)],
                      gx_send.at[d, j], g_recv.at[X - d, 0, j], at_x(d))

    def gc(e):
        return remote(gbuf.at[0, 0], gbuf.at[0, C - e], gc_send.at[e], g_recv.at[0, C - e, 0], at_core(e))

    def gf(d, e, j):
        return remote(gbuf.at[d, 0, :, cols(j)], gbuf.at[d, C - e, :, cols(j)],
                      gf_send.at[d, e, j], g_recv.at[d, C - e, j], at_core(e))

    def kv_up(t, i):
        return remote(kvbuf.at[t, slot(0, (Z - i) % Z)], kvbuf.at[t, slot(0, Z - i - 1)],
                      kvz_send.at[t, 0, i], kv_recv.at[t, 0, Z - i - 1], at_z(1))

    def kv_down(t, i):
        return remote(kvbuf.at[t, slot(0, i)], kvbuf.at[t, slot(0, i + 1)],
                      kvz_send.at[t, 1, i], kv_recv.at[t, 0, i + 1], at_z(Z - 1))

    def goes_up(i):
        return jnp.logical_and(z >= i, z < Z - 1)

    def goes_down(i):
        return jnp.logical_and(z + i <= Z - 1, z > 0)

    def kvy(t, a):
        return remote(kvbuf.at[t, slot(0, 0)], kvbuf.at[t, slot(Y - a, 0)],
                      kvy_send.at[t, a], kv_recv.at[t, Y - a, 0], at_y(a))

    def kvf(t, a, b):
        return remote(kvbuf.at[t, slot(0, b)], kvbuf.at[t, slot(Y - a, b)],
                      kvf_send.at[t, a, b], kv_recv.at[t, Y - a, b], at_y(a))

    def start_kv(t):
        if Z > 1:
            pl.when(goes_up(0))(lambda: kv_up(t, 0).start())
            pl.when(goes_down(0))(lambda: kv_down(t, 0).start())
        for a in range(1, Y):
            kvy(t, a).start()

    loads[0].wait()
    for d in range(1, X):
        gx(d, 0).start()
    loads[2].wait()
    start_kv(0)
    loads[3].wait()
    start_kv(1)
    for e in range(1, C):
        gc(e).start()
    for j in range(1, chunks):
        for d in range(1, X):
            gx(d, j).start()
    loads[1].start()
    for d in range(X):
        for e in range(C):
            if d + e:
                w_load(d, e).start()

    def forward_g(j):
        for d in range(1, X):
            gx(X - d, j).wait_recv()
            for e in range(1, C):
                gf(d, e, j).start()

    def relay_kv(t, i):
        if i > Z - 1:
            return

        @pl.when(z >= i)
        def _():
            kv_up(t, i - 1).wait_recv()
            if i < Z - 1:
                pl.when(z < Z - 1)(lambda: kv_up(t, i).start())
            for a in range(1, Y):
                kvf(t, a, Z - i).start()

        @pl.when(z + i <= Z - 1)
        def _():
            kv_down(t, i - 1).wait_recv()
            if i < Z - 1:
                pl.when(z > 0)(lambda: kv_down(t, i).start())
            for a in range(1, Y):
                kvf(t, a, i).start()

    def arrived_kv(t):
        for a in range(1, Y):
            kvy(t, Y - a).wait_recv()
            for b in range(1, Z):
                kvf(t, Y - a, b).wait_recv()

    def add_chunks(first, last):
        span = slice(first * kc, last * kc)
        total = acc[...]
        for d in range(1, X):
            for e in range(C):
                if e:
                    for j in range(first, last):
                        gf(d, C - e, j).wait_recv()
                total += dot(wbuf[d, e, :, span], gbuf[d, e, :, span], NT)
        acc[...] = total

    def own_block():
        w_load(0, 0).wait()
        acc[...] = dot(wbuf[0, 0], gbuf[0, 0], NT)

    def core_blocks():
        for e in range(1, C):
            gc(C - e).wait_recv()
            w_load(0, e).wait()
            acc[...] += dot(wbuf[0, e], gbuf[0, e], NT)
        for d in range(1, X):
            for e in range(C):
                w_load(d, e).wait()

    lane = lax.broadcasted_iota(jnp.int32, (1, PAIR), 1)
    low = jnp.where(lane < DH, 1.0, 0.0).astype(jnp.bfloat16)
    high = jnp.where(lane < DH, 0.0, 1.0).astype(jnp.bfloat16)
    scale = DH ** -0.5
    row = lax.broadcasted_iota(jnp.int32, (PAIR, 1), 0)
    upper = jnp.where(row < DH, 1.0, 0.0).astype(jnp.bfloat16)
    lower = jnp.where(row < DH, 0.0, 1.0).astype(jnp.bfloat16)

    def at_pair(p):
        return pl.ds(pl.multiple_of(p * PAIR, PAIR), PAIR)

    def both_heads(block):
        return jnp.concatenate((block * low, block * high), axis=0)

    def attention(g, carry):
        members = [g * group + i for i in range(group)]
        queries = [both_heads(qbuf[:, at_pair(p)] * jnp.bfloat16(scale)) for p in members]
        key_pairs = [kvbuf[0, :, at_pair(p)] for p in members]
        scores = [dot(a, b, NT) for a, b in zip(key_pairs, queries)]
        exponents = [jnp.exp(s - jnp.max(s, axis=0, keepdims=True)) for s in scores]
        probs = [e * (1.0 / jnp.sum(e, axis=0, keepdims=True)) for e in exponents]
        for p, q2, key_pair, prob in zip(members, queries, key_pairs, probs):
            q2buf[p] = q2
            ktbuf[p] = key_pair.astype(jnp.float32).T.astype(jnp.bfloat16)
            pbuf[p] = prob
        return carry

    def attend(first, last):
        if first < last:
            lax.fori_loop(first, last, attention, 0)

    mid = (chunks + 1) // 2
    own_block()
    relay_kv(0, 1)
    relay_kv(1, 1)
    core_blocks()
    relay_kv(0, 2)
    forward_g(0)
    relay_kv(1, 2)
    for i in range(3, Z):
        relay_kv(0, i)
    for j in range(1, mid):
        forward_g(j)
    add_chunks(0, mid)
    for i in range(3, Z):
        relay_kv(1, i)
    loads[1].wait()
    arrived_kv(0)
    attend(0, groups // 2)
    for j in range(mid, chunks - 1):
        forward_g(j)
    attend(groups // 2, groups)
    if chunks > 1:
        forward_g(chunks - 1)
    arrived_kv(1)
    for d in range(1, X):
        for e in range(1, C):
            for j in range(mid, chunks):
                gf(d, C - e, j).wait_recv()

    def send1(a, p):
        return remote(s1.at[a - 1, p], r1.at[Y - a - 1, p], s1_send.at[a - 1],
                      r1_recv.at[Y - a - 1, p], at_y(a))

    def send2(b, p):
        return remote(s2.at[b - 1, p], r2.at[Z - b - 1, p], s2_send.at[b - 1],
                      r2_recv.at[Z - b - 1], at_z(b))

    def terms(g):
        members = [g * group + i for i in range(group)]
        inner = pl.ds(pl.multiple_of(g * kc, kc), kc)
        total = acc[inner]
        if mid < chunks:
            span = slice(mid * kc, chunks * kc)
            for d in range(1, X):
                for e in range(C):
                    total += dot(wbuf[d, e, inner, span], gbuf[d, e, :, span], NT)
        head_grads = total.astype(jnp.bfloat16)
        blocks = [head_grads[i * PAIR:(i + 1) * PAIR] for i in range(group)]
        grads = [jnp.concatenate((block * upper, block * lower), axis=1) for block in blocks]
        dps = [dot(kvbuf[1, :, at_pair(p)], do2, NN) for p, do2 in zip(members, grads)]
        probs = [pbuf[p] for p in members]
        lows = [prob.astype(jnp.bfloat16) for prob in probs]
        deltas = [jnp.sum(a.astype(jnp.float32) * b, axis=0, keepdims=True) for a, b in zip(lows, dps)]
        scored = [(a * (b - d)).astype(jnp.bfloat16) for a, b, d in zip(probs, dps, deltas)]
        value_terms = [dot(a, b, NT) for a, b in zip(lows, grads)]
        key_terms = [dot(ds, q2buf[p], NN) for ds, p in zip(scored, members)]
        for p, ds, key_term, value_term in zip(members, scored, key_terms, value_terms):
            dsbuf[p] = ds
            for t, term in enumerate((key_term, value_term)):
                part[p, t] = term[:half]
                for a in range(1, Y):
                    s1[a - 1, p, t] = term[a * half:(a + 1) * half].astype(jnp.bfloat16)
        for p in members:
            for a in range(1, Y):
                send1(a, p).start()

    def second(p):
        for a in range(1, Y):
            send1(Y - a, p).wait_recv()
        for t in range(2):
            total = part[p, t]
            for a in range(1, Y):
                total += r1[a - 1, p, t].astype(jnp.float32)
            part[p, t, :r] = total[:r]
            for b in range(1, Z):
                s2[b - 1, p, t] = total[b * r:(b + 1) * r].astype(jnp.bfloat16)
        for b in range(1, Z):
            send2(b, p).start()

    def query_part(p):
        dqt = dot(ktbuf[p], dsbuf[p], NN)
        both = jnp.concatenate((dqt[:DH, :rows], dqt[DH:, rows:]), axis=0)
        dq_ref[:, at_pair(p)] = (both.T * scale).astype(jnp.bfloat16)

    def relay(g):
        for i in range(group):
            query_part(g * group + i)
            second(g * group + i)

    def first_loop(g, carry):
        terms(g)

        @pl.when(g >= 1)
        def _():
            relay(g - 1)
        return carry

    lax.fori_loop(0, groups, first_loop, 0)
    relay(groups - 1)

    def all1(a):
        return remote(s1.at[a - 1], r1.at[Y - a - 1], s1_send.at[a - 1], r1_recv.at[Y - a - 1, 0], at_y(a))

    def all2(b):
        return remote(s2.at[b - 1], r2.at[Z - b - 1], s2_send.at[b - 1], r2_recv.at[Z - b - 1], at_z(b))

    for b in range(1, Z):
        all2(Z - b).wait_recv()

    for p in range(pairs):
        for t, out in enumerate((dk_ref, dv_ref)):
            total = part[p, t, :r]
            for b in range(1, Z):
                total += r2[b - 1, p, t].astype(jnp.float32)
            out[:, p * PAIR:(p + 1) * PAIR] = total.astype(jnp.bfloat16)
    for a in range(1, Y):
        all1(a).wait_send()
    for b in range(1, Z):
        all2(b).wait_send()

    for j in range(chunks):
        for d in range(1, X):
            gx(d, j).wait_send()
            for e in range(1, C):
                gf(d, e, j).wait_send()
    for e in range(1, C):
        gc(e).wait_send()
    for t in range(2):
        for i in range(Z - 1):
            pl.when(goes_up(i))(lambda: kv_up(t, i).wait_send())
            pl.when(goes_down(i))(lambda: kv_down(t, i).wait_send())
        for b in range(1, Z):
            for a in range(1, Y):
                kvf(t, a, b).wait_send()
        for a in range(1, Y):
            kvy(t, a).wait_send()


def local(n, m, queries, enc_keys, enc_values, grad_out, out_weight):
    rows, width = queries.shape
    r = enc_keys.shape[0]
    Y = inner_extent(n)
    Z = n // Y
    C = 2 if m % 2 == 0 else 1
    X = m // C
    kc = min(256, width)
    pairs = width // PAIR
    chunks = width // kc
    keys, half = n * r, Z * r
    low, full = jnp.bfloat16, jnp.float32
    y1, z1 = max(Y - 1, 1), max(Z - 1, 1)
    dma = pltpu.SemaphoreType.DMA
    vmem = pltpu.VMEM
    return pl.pallas_call(
        functools.partial(kernel, Z, Y, X, C, kc),
        out_shape=(
            pltpu.VMEM((rows, width), low),
            pltpu.VMEM((r, width), low),
            pltpu.VMEM((r, width), low),
        ),
        in_specs=[pl.BlockSpec(memory_space=pl.ANY)] * 5,
        out_specs=[pl.BlockSpec(memory_space=pltpu.VMEM)] * 3,
        scratch_shapes=[
            vmem((rows, width), low),
            vmem((pairs, 2 * rows, PAIR), low),
            vmem((2, keys, width), low),
            vmem((pairs, PAIR, keys), low),
            vmem((X, C, rows, width), low),
            vmem((X, C, width, width), low),
            vmem((width, rows), full),
            vmem((pairs, keys, 2 * rows), full),
            vmem((pairs, keys, 2 * rows), low),
            vmem((pairs, 2, half, PAIR), full),
            vmem((y1, pairs, 2, half, PAIR), low),
            vmem((y1, pairs, 2, half, PAIR), low),
            vmem((z1, pairs, 2, r, PAIR), low),
            vmem((z1, pairs, 2, r, PAIR), low),
            dma((4,)),
            dma((X, C)),
            dma((X, C, chunks)),
            dma((X, chunks)),
            dma((C,)),
            dma((X, C, chunks)),
            dma((2, Y, Z)),
            dma((2, 2, Z)),
            dma((2, Y)),
            dma((2, Y, Z)),
            dma((y1,)),
            dma((y1, pairs)),
            dma((z1,)),
            dma((z1,)),
        ],
        compiler_params=pltpu.CompilerParams(
            collective_id=0, has_side_effects=True, vmem_limit_bytes=62 * 1024 * 1024),
    )(queries, enc_keys, enc_values, grad_out, out_weight)


def solution(mesh):
    return jax.shard_map(
        functools.partial(local, mesh.shape["ctx"], mesh.shape["head"]),
        mesh=mesh,
        in_specs=(
            P("ctx", "head"),
            P("ctx", "head"),
            P("ctx", "head"),
            P("ctx", "head"),
            P("head", None),
        ),
        out_specs=(P("ctx", "head"), P("ctx", "head"), P("ctx", "head")),
        check_vma=False,
    )
```
